32 devices in a mesh: expert: 16 (over z, y, x), dp: 2 (over core).
Axes of the slice: x: 2, y: 2, z: 4, core: 2. Of those that a mesh axis runs over, the one named last changes fastest.
Arguments:
- grad_out: bfloat16 [1024, 1792], P(('expert', 'dp')), may hold values from -6 to 6
- expert_ids: int32 [1024, 8], P(('expert', 'dp')), may hold values from 0 to 15, all different within a row; in each aligned block of 32 rows (0 to 31, 32 to 63, ...) at most 24 rows name the same one
- router_weights: bfloat16 [1024, 8], P(('expert', 'dp')), may hold values from 0.019897461 to 0.29882812
- saved_hidden: bfloat16 [2, 16, 16, 24, 1280], P('dp', 'expert'), may hold values from -0.29882812 to 0.29882812
- down_weight: bfloat16 [16, 1280, 1792], P('expert'), may hold values from -0.15625 to 0.15625
Outputs:
- grad_hidden: bfloat16 [2, 16, 16, 24, 1280], P('dp', 'expert')
- grad_weight: bfloat16 [16, 1280, 1792], P('expert', 'dp')
- grad_router: float32 [1024, 8], P(('expert', 'dp'))
The draws below stay inside these ranges and needn't reach their ends.
Inputs may be any that keep to these rules, and one draw needn't show every extreme that they name: `expert_ids`: each row names 8 different experts. Among the rows held by one device (aligned blocks of 32 rows), no expert is named by more than 24 rows.
All inputs are finite; a program needn't handle non-finite values.
Results may differ from the reference program's by a relative error of at most 0.0058.
Values may be sent and summed in bfloat16 or wider, within the bound.
A program may use at most 64 MiB of HBM per device.

```python
import math
import jax
import jax.numpy as jnp
import numpy as np
from jax import lax

D = 1792
FF = 1280
TOPK = 8
TOK_DEV = 32
EXPERTS = 16
GROUPS = 2
MOST = 24
TOKENS = 1024


def with_spikes(entries, own_key, source, target, shards_of, factor):
    def block_of(dim):
        return (jnp.arange(entries.shape[dim]) // (entries.shape[dim] // shards_of)).reshape((-1,) + (1,) * (entries.ndim - 1 - dim))

    near = jax.random.permutation(own_key, shards_of)[block_of(target)]
    far = (block_of(target) + shards_of // 2) % shards_of
    return jnp.where((block_of(source) == near) | (block_of(source) == far), factor * entries, entries)


def block_levels(rng, dims, cuts, low, top_value):
    def one(dim, shards_of):
        draws = jax.random.uniform(jax.random.fold_in(jax.random.fold_in(rng, 6), dim), (shards_of,), jnp.float32, low / len(cuts), top_value / len(cuts))
        return jnp.repeat(jnp.exp(draws), dims[dim] // shards_of).reshape((-1,) + (1,) * (len(dims) - dim - 1))

    level = one(*cuts[0])
    for cut in cuts[1:]:
        level = level * one(*cut)
    return level


def deal_out(own_key, own, number, rows, amount, top, reach, skew):
    order = jax.random.permutation(own_key, amount)
    crowded, usual = load_shares(amount, rows * top, reach, skew, True), load_shares(amount, rows * top, reach, skew, False)
    places = jnp.arange(amount)

    def named(sizes, offset_by):
        used = int((sizes > 0).sum())
        fixed = max(1, used // 4)
        passed = fixed + (places - fixed + offset_by * (used - fixed)) % max(1, amount - fixed)
        return jnp.zeros((amount,), jnp.int32).at[order[jnp.where(places < fixed, places, passed)]].set(jnp.asarray(sizes, jnp.int32))

    sizes = jnp.where(number % 4 == 0, named(crowded, number // 4), named(usual, number - number // 4 - 1))
    mixed = jax.random.permutation(jax.random.fold_in(own, 3), amount)
    giver, receiver = mixed[0:amount // 2 * 2:2], mixed[1:amount // 2 * 2:2]
    margin = jnp.minimum(sizes[giver] - 1, reach - sizes[receiver]) // 2
    margin = jnp.where((giver == order[0]) | (receiver == order[0]) | (sizes[receiver] == 0), 0, jnp.maximum(margin, 0))
    passed = jax.random.randint(jax.random.fold_in(own, 4), (amount // 2,), 0, 1 << 20) % (margin + 1)
    sizes = sizes.at[giver].add(-passed).at[receiver].add(passed)
    items = jnp.searchsorted(jnp.cumsum(sizes), jnp.arange(rows * top), side="right").astype(jnp.int32)
    table = items.reshape(top, rows).T
    table = table[jax.random.permutation(jax.random.fold_in(own, 1), rows)]
    offset_by = jax.random.randint(jax.random.fold_in(own, 2), (rows, 1), 0, top)
    return jnp.take_along_axis(table, (jnp.arange(top)[None, :] + offset_by) % top, axis=1)


def load_shares(amount, total, reach, lean, full):
    portions = [(1 << 20) // math.isqrt(standing ** lean) + 1 for standing in range(1, amount + 1)]
    largest = reach if full else min(reach, max(-(-total // amount), total * portions[0] // sum(portions)))
    least = 1 if total - largest >= amount - 1 else 0
    counts, spare = [largest] + [least] * (amount - 1), total - largest - least * (amount - 1)
    while spare > 0:
        candidates = [i for i in range(1, amount) if counts[i] < largest] or [i for i in range(1, amount) if counts[i] < reach]
        pool, budget = sum([portions[i] for i in candidates]), spare
        for i in candidates:
            extra = min(reach - counts[i], max(1, budget * portions[i] // pool), spare)
            counts[i] = counts[i] + extra
            spare = spare - extra
    return np.array(counts)


def bell_draw(stream_key, extent, scale, limit, pieces=(), held_as=jnp.bfloat16):
    drawn = scale * jax.random.normal(stream_key, extent, jnp.float32)
    if pieces:
        drawn = drawn * block_levels(stream_key, extent, pieces, -0.22, 0.18)
    return jnp.clip(drawn, -limit, limit).astype(held_as)


def heavy_noise(key, extent, width, reach, shards, heavy, held_as=jnp.bfloat16):
    drawn = width * jax.random.normal(key, extent, jnp.float32)
    if shards:
        drawn = drawn * block_levels(key, extent, shards, -0.22, 0.18)
    return jnp.clip(with_spikes(drawn, jax.random.fold_in(key, 3), *heavy), -reach, reach).astype(held_as)


def setup_inputs(seed: int = 0) -> dict:
    keys = jax.random.split(jax.random.key(seed), 6)
    grad_out = bell_draw(keys[0], (TOKENS, D), 1.0, 6.0, ((0, 32),))
    expert_ids_keys = jax.random.split(jax.random.fold_in(keys[1], 1), TOKENS // TOK_DEV)
    expert_ids_turns = jax.random.permutation(jax.random.fold_in(keys[1], 3), TOKENS // TOK_DEV)
    expert_ids = jax.vmap(lambda own, number: deal_out(jax.random.fold_in(keys[1], 2), own, number, TOK_DEV, EXPERTS, TOPK, MOST, 2))(expert_ids_keys, expert_ids_turns).reshape((TOKENS, TOPK))
    router_weights = jnp.clip(0.019897461 + 0.27893066 * jax.random.uniform(keys[2], (TOKENS, TOPK), jnp.float32) ** block_levels(keys[2], (TOKENS, TOPK), ((0, 32),), -0.2, 0.2), 0.019897461, 0.29882812).astype(jnp.bfloat16)
    saved_hidden = heavy_noise(keys[3], (GROUPS, EXPERTS, EXPERTS, MOST, FF), 0.05, 0.29882812, ((0, 2), (1, 16)), (0, 4, 2, 2.0))
    down_weight = bell_draw(keys[4], (EXPERTS, FF, D), FF ** -0.5, 0.15625, ((0, 16),))
    return {"grad_out": grad_out, "expert_ids": expert_ids, "router_weights": router_weights, "saved_hidden": saved_hidden, "down_weight": down_weight}


def slot_table(ids):
    flat_ids = ids.reshape(-1)
    onehot = (flat_ids[:, None] == jnp.arange(EXPERTS, dtype=jnp.int32)[None, :]).astype(jnp.int32)
    slot_rank = jnp.sum((jnp.cumsum(onehot, axis=0) - onehot) * onehot, axis=1)
    return (flat_ids * MOST + slot_rank).astype(jnp.int32)


def dispatch(grad_block, weight_block, ids):
    slot_index = slot_table(ids)
    token_rows = jnp.repeat(grad_block, TOPK, axis=0)
    outgoing = jnp.zeros((EXPERTS * MOST, D), jnp.bfloat16).at[slot_index].set(token_rows)
    scales = jnp.zeros((EXPERTS * MOST,), jnp.bfloat16).at[slot_index].set(weight_block.reshape(-1))
    return outgoing.reshape(EXPERTS, MOST, D), scales.reshape(EXPERTS, MOST), slot_index


def owner_work(packed):
    arrived, scales, hidden, weight = packed
    token_rows = arrived.reshape(-1, D)
    hidden_rows = hidden.reshape(-1, FF)
    row_scale = scales.reshape(-1).astype(jnp.float32)
    projected = jnp.dot(token_rows, weight.T, preferred_element_type=jnp.float32)
    grad_hid = (row_scale[:, None] * projected).astype(jnp.bfloat16).reshape(EXPERTS, MOST, FF)
    prob_grad = jnp.sum(hidden_rows.astype(jnp.float32) * projected, axis=1).reshape(EXPERTS, MOST)
    scaled = (row_scale[:, None] * token_rows.astype(jnp.float32)).astype(jnp.bfloat16)
    partial_value = jnp.dot(hidden_rows.T, scaled, preferred_element_type=jnp.float32).astype(jnp.bfloat16)
    return grad_hid, prob_grad, partial_value


def pick_rows(returned_row, slot_row):
    return returned_row[slot_row]


def reference(grad_out, expert_ids, router_weights, saved_hidden, down_weight):
    def group_step(running, inputs):
        grad_group, ids_group, weights_group, hidden_group = inputs
        outgoing, scales, slot_index = jax.vmap(dispatch)(grad_group, weights_group, ids_group)
        outgoing = jnp.swapaxes(outgoing, 0, 1)
        scales = jnp.swapaxes(scales, 0, 1)
        grad_hid, prob_grad, partial_value = lax.map(owner_work, (outgoing, scales, hidden_group, down_weight))
        returned = jnp.swapaxes(prob_grad, 0, 1).reshape(EXPERTS, EXPERTS * MOST)
        router = jax.vmap(pick_rows)(returned, slot_index).reshape(EXPERTS, TOK_DEV, TOPK)
        return running + partial_value.astype(jnp.float32), (grad_hid, router)

    grad_groups = jnp.swapaxes(grad_out.reshape(EXPERTS, GROUPS, TOK_DEV, D), 0, 1)
    ids_groups = jnp.swapaxes(expert_ids.reshape(EXPERTS, GROUPS, TOK_DEV, TOPK), 0, 1)
    weight_groups = jnp.swapaxes(router_weights.reshape(EXPERTS, GROUPS, TOK_DEV, TOPK), 0, 1)
    start = jnp.zeros((EXPERTS, FF, D), jnp.float32)
    running, (grad_hidden, router) = lax.scan(group_step, start, (grad_groups, ids_groups, weight_groups, saved_hidden))
    grad_weight = running.astype(jnp.bfloat16)
    grad_router = jnp.swapaxes(router, 0, 1).reshape(TOKENS, TOPK)
    return grad_hidden, grad_weight, grad_router
```

```python
import jax
import jax.numpy as jnp
from jax import lax
from jax.experimental import pallas as pl
from jax.experimental.pallas import tpu as pltpu
from jax.sharding import PartitionSpec as P


def on_device(grad_out, expert_ids, router_weights, saved_hidden, down_weight):
    experts = lax.axis_size("expert")
    groups = lax.axis_size("dp")
    token_count = grad_out.shape[0]
    top_count = expert_ids.shape[1]
    capacity = saved_hidden.shape[3]
    features = grad_out.shape[1]
    hidden_units = saved_hidden.shape[4]
    flat_ids = expert_ids.reshape(-1)
    onehot = (flat_ids[:, None] == jnp.arange(experts, dtype=jnp.int32)[None, :]).astype(jnp.int32)
    slot_rank = jnp.sum((jnp.cumsum(onehot, axis=0) - onehot) * onehot, axis=1)
    slot_index = flat_ids * capacity + slot_rank
    token_rows = jnp.repeat(grad_out, top_count, axis=0)
    outgoing = (
        jnp.zeros((experts * capacity, features), jnp.bfloat16).at[slot_index].set(token_rows)
    )
    outgoing = outgoing.reshape(experts, capacity, features)
    scales_out = (
        jnp.zeros((experts * capacity,), jnp.bfloat16)
        .at[slot_index]
        .set(router_weights.reshape(-1))
    )
    scales_out = scales_out.reshape(experts, capacity)
    arrived, arrived_scales = (
        lax.all_to_all(outgoing, "expert", split_axis=0, concat_axis=0, tiled=True),
        lax.all_to_all(scales_out, "expert", split_axis=0, concat_axis=0, tiled=True),
    )
    slot_rows = arrived.reshape(experts * capacity, features)
    row_scale = arrived_scales.reshape(-1).astype(jnp.float32)
    hidden_rows = saved_hidden.reshape(experts * capacity, hidden_units)
    weight = down_weight[0]
    projected = lax.dot_general(
        slot_rows, weight, (((1,), (1,)), ((), ())), preferred_element_type=jnp.float32
    )
    grad_hidden = (row_scale[:, None] * projected).astype(jnp.bfloat16)
    grad_hidden = grad_hidden.reshape(1, 1, experts, capacity, hidden_units)
    prob_grad = jnp.sum(hidden_rows.astype(jnp.float32) * projected, axis=1).reshape(
        experts, capacity
    )
    returned = lax.all_to_all(prob_grad, "expert", split_axis=0, concat_axis=0, tiled=True)
    grad_router = returned.reshape(-1)[slot_index].reshape(token_count, top_count)
    scaled = (row_scale[:, None] * slot_rows.astype(jnp.float32)).astype(jnp.bfloat16)
    own_rows = hidden_units // groups
    weight_term = lax.dot_general(
        hidden_rows, scaled, (((0,), (0,)), ((), ())), preferred_element_type=jnp.float32
    )
    weight_term = weight_term.astype(jnp.bfloat16).astype(jnp.float32)
    summed = lax.psum_scatter(
        weight_term.astype(jnp.bfloat16), "dp", scatter_dimension=0, tiled=True
    )
    grad_weight = summed.reshape(1, own_rows, features)
    return (grad_hidden, grad_weight, grad_router)


MESH = pl.DeviceIdType.MESH
META = 128
TILE = 256


def inverse(j):
    return (j // 4) * 4 + (4 - j % 4) % 4


def fused_kernel(
    ids_ref, rw_ref, go_hbm, hid_hbm, w_hbm,
    gh_hbm, gw_hbm, gr_ref,
    tok, hid, wv, x, sc, hid_t, hid_out, gh, gw, msg, ret,
    go_sem, hid_sem, w_sem, gh_sem, gw_sem,
    tok_send, tok_recv, hid_send, hid_recv, sc_send, sc_recv, ret_send, ret_recv,
):
    f32, bf16 = jnp.float32, jnp.bfloat16
    tokens, features = go_hbm.shape
    capacity, hidden_units = hid.shape[1], hid.shape[2]
    half = hidden_units // 2
    slots = 8 * capacity
    rows = 8 * tokens
    me = lax.axis_index("expert")
    g = lax.axis_index("dp")
    stride_a, stride_b = 1 + g, 2 - g
    step_a = stride_a * (1 - 2 * ((me // stride_a) % 2))
    step_b = stride_b * (1 - 2 * ((me // stride_b) % 2))
    base = (me, me + step_a, me + step_b, me + step_a + step_b)
    source = [lax.rem(base[j // 4] + 16 - 4 * (j % 4), 16) for j in range(16)]
    next_a, next_b = base[1], base[2]

    load_go = pltpu.make_async_copy(go_hbm, tok.at[pl.ds(0, tokens), pl.ds(0, features)], go_sem)
    load_go.start()
    load_hid = []
    for j in range(16):
        load_hid.append(pltpu.make_async_copy(hid_hbm.at[source[j]], hid.at[j], hid_sem.at[j]))
        load_hid[j].start()
    load_w = pltpu.make_async_copy(w_hbm, wv, w_sem)
    load_w.start()

    barrier = pltpu.get_barrier_semaphore()
    for j in range(1, 16):
        pl.semaphore_signal(barrier, inc=1, device_id=(source[j], g), device_id_type=MESH)
    pl.semaphore_signal(barrier, inc=1, device_id=(me, 1 - g), device_id_type=MESH)

    ids = ids_ref[...]
    rw = rw_ref[...].astype(f32)
    lane = lax.broadcasted_iota(jnp.int32, (tokens, META), 1)
    expert = lane % 16
    weight = jnp.zeros((tokens, META), f32)
    routed = jnp.zeros((tokens, META), f32)
    for k in range(ids.shape[1]):
        hit = ids[:, k : k + 1] == expert
        weight += jnp.where(hit, rw[:, k : k + 1], 0.0)
        routed += jnp.where(hit, 1.0, 0.0)
    earlier = lax.broadcasted_iota(jnp.int32, (tokens, tokens), 1) < lax.broadcasted_iota(
        jnp.int32, (tokens, tokens), 0
    )
    rank = jnp.dot(
        jnp.where(earlier, 1.0, 0.0).astype(bf16), routed.astype(bf16), preferred_element_type=f32
    )
    rank = jnp.where(routed > 0.0, rank + 1.0, 0.0)
    meta = jnp.where(lane < 16, weight, jnp.where(lane < 32, rank, 0.0))
    tok[pl.ds(0, tokens), pl.ds(features, META)] = meta.astype(bf16)
    msg[...] = jnp.zeros_like(msg)
    load_go.wait()
    pl.semaphore_wait(barrier, 16)

    def send_block(src, dst, device, sem):
        copy = pltpu.make_async_remote_copy(
            src_ref=tok.at[pl.ds(src * tokens, tokens)],
            dst_ref=tok.at[pl.ds(dst * tokens, tokens)],
            send_sem=tok_send.at[sem],
            recv_sem=tok_recv.at[dst],
            device_id=(device, g),
            device_id_type=MESH,
        )
        copy.start()
        return copy

    copies = [None] * 16
    copies[4] = send_block(0, 4, next_a, 4)
    copies[8] = send_block(0, 8, next_b, 8)
    for d in (1, 3, 2):
        copies[d] = send_block(0, d, source[inverse(d)], d)

    for j in range(16):
        load_hid[j].wait()

    def turn(i, carry):
        at = pl.multiple_of(i * 128, 128)
        mine = pl.multiple_of(g * half + i * 128, 128)
        other = pl.multiple_of((1 - g) * half + i * 128, 128)
        for col, ref in ((other, hid_out), (mine, hid_t)):
            part = hid[:, :, pl.ds(col, 128)].astype(f32).reshape(2 * slots, 128)
            ref[pl.ds(at, 128), pl.ds(0, 2 * slots)] = part.T.astype(bf16)
        return carry

    lax.fori_loop(0, half // 128, turn, 0)
    swap_hid = pltpu.make_async_remote_copy(
        src_ref=hid_out,
        dst_ref=hid_t.at[:, pl.ds(2 * slots, 2 * slots)],
        send_sem=hid_send,
        recv_sem=hid_recv,
        device_id=(me, 1 - g),
        device_id_type=MESH,
    )
    swap_hid.start()

    for d in (1, 3, 2):
        copies[d].wait_recv()
        copies[4 + d] = send_block(d, 4 + d, next_a, 4 + d)
        copies[8 + d] = send_block(d, 8 + d, next_b, 8 + d)
    for d in (0, 1, 3, 2):
        copies[4 + d].wait_recv()
        copies[12 + d] = send_block(4 + d, 12 + d, next_b, 12 + d)
    load_w.wait()

    back = [None] * 16
    stores = []
    swaps = []

    def work(part):
        at = part * rows
        lanes = lax.broadcasted_iota(jnp.int32, (rows, META), 1)
        held = tok[pl.ds(at, rows), pl.ds(features, META)].astype(f32)
        rank1 = jnp.sum(jnp.where(lanes == me + 16, held, 0.0), axis=1, keepdims=True)
        row = lax.broadcasted_iota(jnp.int32, (rows, 1), 0)
        first = ((row // tokens) * capacity).astype(f32)
        target = jnp.where(rank1 > 0.0, first + rank1 - 1.0, -1.0)
        eye = lax.broadcasted_iota(jnp.int32, (rows, rows), 0) == lax.broadcasted_iota(
            jnp.int32, (rows, rows), 1
        )
        target = jnp.sum(jnp.where(eye, target, 0.0), axis=0, keepdims=True)
        slot = lax.broadcasted_iota(jnp.int32, (slots, rows), 0).astype(f32)
        chosen = slot == target
        pick = jnp.where(chosen, 1.0, 0.0).astype(bf16)
        slot_meta = jnp.dot(
            pick, tok[pl.ds(at, rows), pl.ds(features, META)], preferred_element_type=f32
        )
        lanes = lax.broadcasted_iota(jnp.int32, (slots, META), 1)
        scale = jnp.sum(jnp.where(lanes == me, slot_meta, 0.0), axis=1, keepdims=True)
        for i in range(features // TILE):
            cols = pl.ds(i * TILE, TILE)
            moved = jnp.dot(pick, tok[pl.ds(at, rows), cols], preferred_element_type=f32)
            x[:, cols] = moved.astype(bf16)
            sc[pl.ds(part * slots, slots), cols] = (scale * moved).astype(bf16)
        swap = pltpu.make_async_remote_copy(
            src_ref=sc.at[pl.ds(part * slots, slots)],
            dst_ref=sc.at[pl.ds((2 + part) * slots, slots)],
            send_sem=sc_send.at[part],
            recv_sem=sc_recv.at[part],
            device_id=(me, 1 - g),
            device_id_type=MESH,
        )
        swap.start()
        swaps.append(swap)
        prob = jnp.zeros((slots, 1), f32)
        for i in range(hidden_units // TILE):
            cols = pl.ds(i * TILE, TILE)
            projected = lax.dot_general(
                x[...], wv[cols, :], (((1,), (1,)), ((), ())), preferred_element_type=f32
            )
            saved = hid[pl.ds(8 * part, 8), :, cols].astype(f32).reshape(slots, TILE)
            prob += jnp.sum(saved * projected, axis=1, keepdims=True)
            gh[pl.ds(8 * part, 8), :, cols] = (
                (scale * projected).reshape(8, capacity, TILE).astype(bf16)
            )
        by_token = jnp.sum(jnp.where(chosen, prob, 0.0), axis=0, keepdims=True)
        for i in range(8):
            j = 8 * part + i
            mine = by_token[:, tokens * i : tokens * (i + 1)]
            if j == 0:
                ret[0, 0:1, 0:tokens] = mine
            else:
                msg[j, 0:1, 0:tokens] = mine
        for i in range(8):
            j = 8 * part + i
            if j > 0:
                back[j] = pltpu.make_async_remote_copy(
                    src_ref=msg.at[j],
                    dst_ref=ret.at[inverse(j)],
                    send_sem=ret_send.at[j],
                    recv_sem=ret_recv.at[inverse(j)],
                    device_id=(source[j], g),
                    device_id_type=MESH,
                )
                back[j].start()
        for i in range(8):
            j = 8 * part + i
            store = pltpu.make_async_copy(gh.at[j], gh_hbm.at[source[j]], gh_sem.at[j])
            store.start()
            stores.append(store)

    work(0)
    for j in (8, 9, 11, 10, 12, 13, 15, 14):
        copies[j].wait_recv()
    work(1)

    swap_hid.wait_recv()
    for swap in swaps:
        swap.wait_recv()
    for i in range(features // TILE):
        cols = pl.ds(i * TILE, TILE)
        gw[:, cols] = jnp.dot(hid_t[...], sc[:, cols], preferred_element_type=f32).astype(bf16)
        store = pltpu.make_async_copy(gw.at[:, cols], gw_hbm.at[:, cols], gw_sem.at[i])
        store.start()
        stores.append(store)

    eye = lax.broadcasted_iota(jnp.int32, (tokens, tokens), 0) == lax.broadcasted_iota(
        jnp.int32, (tokens, tokens), 1
    )
    total = jnp.zeros(ids.shape, f32)
    for j in range(16):
        if j > 0:
            back[inverse(j)].wait_recv()
        column = jnp.sum(jnp.where(eye, ret[j, 0:1, 0:tokens], 0.0), axis=1, keepdims=True)
        total += jnp.where(ids == source[j], column, 0.0)
    gr_ref[...] = total

    for j in range(1, 16):
        copies[j].wait_send()
        back[j].wait_send()
    swap_hid.wait_send()
    for swap in swaps:
        swap.wait_send()
    for store in stores:
        store.wait()


def on_pair(grad_out, expert_ids, router_weights, saved_hidden, down_weight):
    tokens, features = grad_out.shape
    _, _, experts, capacity, hidden_units = saved_hidden.shape
    half = hidden_units // 2
    slots = experts * capacity
    bf16, f32 = jnp.bfloat16, jnp.float32
    dma = pltpu.SemaphoreType.DMA
    vmem = pl.BlockSpec(memory_space=pltpu.VMEM)
    hbm = pl.BlockSpec(memory_space=pl.ANY)
    grad_hidden, grad_weight, grad_router = pl.pallas_call(
        fused_kernel,
        out_shape=(
            jax.ShapeDtypeStruct((experts, capacity, hidden_units), bf16),
            jax.ShapeDtypeStruct((half, features), bf16),
            jax.ShapeDtypeStruct(expert_ids.shape, f32),
        ),
        in_specs=[vmem, vmem, hbm, hbm, hbm],
        out_specs=(hbm, hbm, vmem),
        scratch_shapes=[
            pltpu.VMEM((experts * tokens, features + META), bf16),
            pltpu.VMEM((experts, capacity, hidden_units), bf16),
            pltpu.VMEM((hidden_units, features), bf16),
            pltpu.VMEM((slots // 2, features), bf16),
            pltpu.VMEM((2 * slots, features), bf16),
            pltpu.VMEM((half, 2 * slots), bf16),
            pltpu.VMEM((half, slots), bf16),
            pltpu.VMEM((experts, capacity, hidden_units), bf16),
            pltpu.VMEM((half, features), bf16),
            pltpu.VMEM((experts, 8, 128), f32),
            pltpu.VMEM((experts, 8, 128), f32),
            dma,
            dma((16,)),
            dma,
            dma((16,)),
            dma((features // TILE,)),
            dma((16,)),
            dma((16,)),
            dma,
            dma,
            dma((2,)),
            dma((2,)),
            dma((16,)),
            dma((16,)),
        ],
        compiler_params=pltpu.CompilerParams(
            collective_id=0, has_side_effects=True, vmem_limit_bytes=48 * 1024 * 1024
        ),
        cost_estimate=pl.CostEstimate(
            flops=4 * slots * hidden_units * features,
            bytes_accessed=10_000_000,
            transcendentals=0,
        ),
    )(expert_ids, router_weights, grad_out, saved_hidden[0, 0], down_weight[0])
    return grad_hidden[None, None], grad_weight[None], grad_router


def solution(mesh):
    fused = mesh.shape["expert"] == 16 and mesh.shape["dp"] == 2
    placed = (
        P(("expert", "dp"), None),
        P(("expert", "dp"), None),
        P(("expert", "dp"), None),
        P("dp", "expert", None, None, None),
        P("expert", None, None),
    )
    return jax.shard_map(
        on_pair if fused else on_device,
        mesh=mesh,
        in_specs=placed,
        out_specs=(
            P("dp", "expert", None, None, None),
            P("expert", "dp", None),
            P(("expert", "dp"), None),
        ),
        check_vma=False,
    )
```

```python
import jax
import jax.numpy as jnp
from jax import lax
from jax.experimental import pallas as pl
from jax.experimental.pallas import tpu as pltpu
from jax.sharding import PartitionSpec as P


def on_device(grad_out, expert_ids, router_weights, saved_hidden, down_weight):
    experts = lax.axis_size("expert")
    groups = lax.axis_size("dp")
    token_count = grad_out.shape[0]
    top_count = expert_ids.shape[1]
    capacity = saved_hidden.shape[3]
    features = grad_out.shape[1]
    hidden_units = saved_hidden.shape[4]
    flat_ids = expert_ids.reshape(-1)
    onehot = (flat_ids[:, None] == jnp.arange(experts, dtype=jnp.int32)[None, :]).astype(jnp.int32)
    slot_rank = jnp.sum((jnp.cumsum(onehot, axis=0) - onehot) * onehot, axis=1)
    slot_index = flat_ids * capacity + slot_rank
    token_rows = jnp.repeat(grad_out, top_count, axis=0)
    outgoing = (
        jnp.zeros((experts * capacity, features), jnp.bfloat16).at[slot_index].set(token_rows)
    )
    outgoing = outgoing.reshape(experts, capacity, features)
    scales_out = (
        jnp.zeros((experts * capacity,), jnp.bfloat16)
        .at[slot_index]
        .set(router_weights.reshape(-1))
    )
    scales_out = scales_out.reshape(experts, capacity)
    arrived, arrived_scales = (
        lax.all_to_all(outgoing, "expert", split_axis=0, concat_axis=0, tiled=True),
        lax.all_to_all(scales_out, "expert", split_axis=0, concat_axis=0, tiled=True),
    )
    slot_rows = arrived.reshape(experts * capacity, features)
    row_scale = arrived_scales.reshape(-1).astype(jnp.float32)
    hidden_rows = saved_hidden.reshape(experts * capacity, hidden_units)
    weight = down_weight[0]
    projected = lax.dot_general(
        slot_rows, weight, (((1,), (1,)), ((), ())), preferred_element_type=jnp.float32
    )
    grad_hidden = (row_scale[:, None] * projected).astype(jnp.bfloat16)
    grad_hidden = grad_hidden.reshape(1, 1, experts, capacity, hidden_units)
    prob_grad = jnp.sum(hidden_rows.astype(jnp.float32) * projected, axis=1).reshape(
        experts, capacity
    )
    returned = lax.all_to_all(prob_grad, "expert", split_axis=0, concat_axis=0, tiled=True)
    grad_router = returned.reshape(-1)[slot_index].reshape(token_count, top_count)
    scaled = (row_scale[:, None] * slot_rows.astype(jnp.float32)).astype(jnp.bfloat16)
    own_rows = hidden_units // groups
    weight_term = lax.dot_general(
        hidden_rows, scaled, (((0,), (0,)), ((), ())), preferred_element_type=jnp.float32
    )
    weight_term = weight_term.astype(jnp.bfloat16).astype(jnp.float32)
    summed = lax.psum_scatter(
        weight_term.astype(jnp.bfloat16), "dp", scatter_dimension=0, tiled=True
    )
    grad_weight = summed.reshape(1, own_rows, features)
    return (grad_hidden, grad_weight, grad_router)


MESH = pl.DeviceIdType.MESH
META = 128
TILE = 256


def inverse(j):
    return (j // 4) * 4 + (4 - j % 4) % 4


def fused_kernel(
    ids_ref, rw_ref, go_hbm, hid_hbm, w_hbm,
    gh_hbm, gw_hbm, gr_ref,
    tok, hid, wv, x, sc, hid_own, hid_sib, hid_out, acc, gh, gw, msg, ret,
    go_sem, hid_sem, w_sem, gh_sem, gw_sem,
    tok_send, tok_recv, z_send, hid_send, hid_recv, sc_send, sc_recv, ret_send, ret_recv,
):
    f32, bf16 = jnp.float32, jnp.bfloat16
    tokens, features = go_hbm.shape
    capacity, hidden_units = hid.shape[1], hid.shape[2]
    half = hidden_units // 2
    slots = 8 * capacity
    rows = 8 * tokens
    me = lax.axis_index("expert")
    g = lax.axis_index("dp")
    stride_a, stride_b = 1 + g, 2 - g
    step_a = stride_a * (1 - 2 * ((me // stride_a) % 2))
    step_b = stride_b * (1 - 2 * ((me // stride_b) % 2))
    base = (me, me + step_a, me + step_b, me + step_a + step_b)
    source = [lax.rem(base[j // 4] + 16 - 4 * (j % 4), 16) for j in range(16)]
    next_a, next_b = base[1], base[2]

    barrier = pltpu.get_barrier_semaphore()
    for j in range(1, 16):
        pl.semaphore_signal(barrier, inc=1, device_id=(source[j], g), device_id_type=MESH)
    pl.semaphore_signal(barrier, inc=1, device_id=(me, 1 - g), device_id_type=MESH)

    load_go = pltpu.make_async_copy(go_hbm, tok.at[pl.ds(0, tokens), pl.ds(0, features)], go_sem)
    load_go.start()
    load_hid = []
    for j in range(16):
        load_hid.append(pltpu.make_async_copy(hid_hbm.at[source[j]], hid.at[j], hid_sem.at[j]))
        load_hid[j].start()
    load_w = pltpu.make_async_copy(w_hbm, wv, w_sem)
    load_w.start()

    ids = ids_ref[...]
    rw = rw_ref[...].astype(f32)
    place = lax.broadcasted_iota(jnp.int32, (META, tokens), 0)
    expert = place % 16
    weight = jnp.zeros((META, tokens), f32)
    routed = jnp.zeros((META, tokens), f32)
    for k in range(ids.shape[0]):
        hit = ids[k : k + 1, :] == expert
        weight += jnp.where(hit, rw[k : k + 1, :], 0.0)
        routed += jnp.where(hit, 1.0, 0.0)
    one = lax.broadcasted_iota(jnp.int32, (tokens, tokens), 0)
    two = lax.broadcasted_iota(jnp.int32, (tokens, tokens), 1)
    rank = jnp.dot(
        routed.astype(bf16), jnp.where(one < two, 1.0, 0.0).astype(bf16), preferred_element_type=f32
    )
    rank = jnp.where(routed > 0.0, rank + 1.0, 0.0)
    meta = jnp.where(place < 16, weight, jnp.where(place < 32, rank, 0.0))
    meta = lax.dot_general(
        jnp.where(one == two, 1.0, 0.0).astype(bf16),
        meta.astype(bf16),
        (((1,), (1,)), ((), ())),
        preferred_element_type=f32,
    )
    tok[pl.ds(0, tokens), pl.ds(features, META)] = meta.astype(bf16)
    msg[...] = jnp.zeros_like(msg)
    load_go.wait()
    pl.semaphore_wait(barrier, 16)

    def block(src, dst, device, sem):
        return pltpu.make_async_remote_copy(
            src_ref=tok.at[pl.ds(pl.multiple_of(src * tokens, tokens), tokens)],
            dst_ref=tok.at[pl.ds(pl.multiple_of(dst * tokens, tokens), tokens)],
            send_sem=sem,
            recv_sem=tok_recv.at[dst],
            device_id=(device, g),
            device_id_type=MESH,
        )

    def over_a(d):
        return block(d, 4 + d, next_a, tok_send.at[4 + d])

    def over_b(j):
        return block(j, 8 + j, next_b, tok_send.at[8 + j])

    z = me // 4
    first, last = 1 - (z + 3) // 4, z // 3
    order = (1 + 2 * first, 3 - first - last, 2 + last - first)

    def along_z(act):
        @pl.when(z < 3)
        def _():
            act(block(0, 1, me + 4, z_send.at[0]))

        @pl.when(z > 0)
        def _():
            act(block(0, 3, me - 4, z_send.at[4]))

    def pass_on(d, act):
        @pl.when(jnp.logical_and(d <= z, z < 3))
        def _():
            act(block(d, d + 1, me + 4, z_send.at[d]))

        @pl.when(jnp.logical_and(d > z, z > 0))
        def _():
            act(block(d, d - 1, me - 4, z_send.at[d]))

    along_z(lambda copy: copy.start())
    over_a(0).start()
    over_b(0).start()

    for j in range(16):
        load_hid[j].wait()

    def turn(i, carry):
        at = pl.multiple_of(i * 128, 128)
        mine = pl.multiple_of(g * half + i * 128, 128)
        other = pl.multiple_of((1 - g) * half + i * 128, 128)
        for part in range(2):
            for col, ref in ((other, hid_out), (mine, hid_own)):
                piece = hid[pl.ds(8 * part, 8), :, pl.ds(col, 128)].astype(f32).reshape(slots, 128)
                ref[part, pl.ds(at, 128), :] = piece.T.astype(bf16)
        return carry

    lax.fori_loop(0, half // 128, turn, 0)
    swap_hid = pltpu.make_async_remote_copy(
        src_ref=hid_out,
        dst_ref=hid_sib,
        send_sem=hid_send,
        recv_sem=hid_recv,
        device_id=(me, 1 - g),
        device_id_type=MESH,
    )
    swap_hid.start()

    before = 0
    for d in order:
        block(0, d, next_a, tok_send.at[0]).wait_recv()
        pass_on(d, lambda copy: copy.start())
        over_a(d).start()
        over_b(d).start()
        over_a(before).wait_recv()
        over_b(4 + before).start()
        before = d
    over_a(before).wait_recv()
    over_b(4 + before).start()
    load_w.wait()

    back = [None] * 16
    stores = []
    swaps = []

    def work(part):
        at = part * rows
        lanes = lax.broadcasted_iota(jnp.int32, (rows, META), 1)
        held = tok[pl.ds(at, rows), pl.ds(features, META)].astype(f32)
        rank1 = jnp.sum(jnp.where(lanes == me + 16, held, 0.0), axis=1, keepdims=True)
        row = lax.broadcasted_iota(jnp.int32, (rows, 1), 0)
        first = ((row // tokens) * capacity).astype(f32)
        target = jnp.where(rank1 > 0.0, first + rank1 - 1.0, -1.0)
        eye = lax.broadcasted_iota(jnp.int32, (rows, rows), 0) == lax.broadcasted_iota(
            jnp.int32, (rows, rows), 1
        )
        target = jnp.sum(jnp.where(eye, target, 0.0), axis=0, keepdims=True)
        slot = lax.broadcasted_iota(jnp.int32, (slots, rows), 0).astype(f32)
        chosen = slot == target
        pick = jnp.where(chosen, 1.0, 0.0).astype(bf16)
        slot_meta = jnp.dot(
            pick, tok[pl.ds(at, rows), pl.ds(features, META)], preferred_element_type=f32
        )
        lanes = lax.broadcasted_iota(jnp.int32, (slots, META), 1)
        scale = jnp.sum(jnp.where(lanes == me, slot_meta, 0.0), axis=1, keepdims=True)
        for i in range(features // TILE):
            cols = pl.ds(i * TILE, TILE)
            moved = jnp.dot(pick, tok[pl.ds(at, rows), cols], preferred_element_type=f32)
            x[:, cols] = moved.astype(bf16)
            sc[pl.ds(part * slots, slots), cols] = (scale * moved).astype(bf16)
        swap = pltpu.make_async_remote_copy(
            src_ref=sc.at[pl.ds(part * slots, slots)],
            dst_ref=sc.at[pl.ds((2 + part) * slots, slots)],
            send_sem=sc_send.at[part],
            recv_sem=sc_recv.at[part],
            device_id=(me, 1 - g),
            device_id_type=MESH,
        )
        swap.start()
        swaps.append(swap)
        prob = jnp.zeros((slots, 1), f32)
        for i in range(hidden_units // TILE):
            cols = pl.ds(i * TILE, TILE)
            projected = lax.dot_general(
                x[...], wv[cols, :], (((1,), (1,)), ((), ())), preferred_element_type=f32
            )
            saved = hid[pl.ds(8 * part, 8), :, cols].astype(f32).reshape(slots, TILE)
            prob += jnp.sum(saved * projected, axis=1, keepdims=True)
            gh[pl.ds(8 * part, 8), :, cols] = (
                (scale * projected).reshape(8, capacity, TILE).astype(bf16)
            )
        by_token = jnp.sum(jnp.where(chosen, prob, 0.0), axis=0, keepdims=True)
        for i in range(8):
            j = 8 * part + i
            mine = by_token[:, tokens * i : tokens * (i + 1)]
            if j == 0:
                ret[0, 0:1, 0:tokens] = mine
            else:
                msg[j, 0:1, 0:tokens] = mine
        for i in range(8):
            j = 8 * part + i
            if j > 0:
                back[j] = pltpu.make_async_remote_copy(
                    src_ref=msg.at[j],
                    dst_ref=ret.at[inverse(j)],
                    send_sem=ret_send.at[j],
                    recv_sem=ret_recv.at[inverse(j)],
                    device_id=(source[j], g),
                    device_id_type=MESH,
                )
                back[j].start()
        for i in range(8):
            j = 8 * part + i
            store = pltpu.make_async_copy(gh.at[j], gh_hbm.at[source[j]], gh_sem.at[j])
            store.start()
            stores.append(store)

    def weight_part(part, cols):
        return jnp.dot(
            hid_own[part], sc[pl.ds(part * slots, slots), cols], preferred_element_type=f32
        ) + jnp.dot(
            hid_sib[part], sc[pl.ds((2 + part) * slots, slots), cols], preferred_element_type=f32
        )

    work(0)
    swap_hid.wait_recv()
    swaps[0].wait_recv()
    for i in range(features // TILE):
        cols = pl.ds(i * TILE, TILE)
        acc[:, cols] = weight_part(0, cols)
    for j in range(8):
        over_b(j).wait_recv()
    work(1)
    swaps[1].wait_recv()
    for i in range(features // TILE):
        cols = pl.ds(i * TILE, TILE)
        gw[:, cols] = (acc[:, cols] + weight_part(1, cols)).astype(bf16)
        store = pltpu.make_async_copy(gw.at[:, cols], gw_hbm.at[:, cols], gw_sem.at[i])
        store.start()
        stores.append(store)

    total = jnp.zeros(ids.shape, f32)
    for j in range(16):
        if j > 0:
            back[inverse(j)].wait_recv()
        total += jnp.where(ids == source[j], ret[j, 0:1, 0:tokens], 0.0)
    gr_ref[...] = total

    along_z(lambda copy: copy.wait_send())
    for d in order:
        pass_on(d, lambda copy: copy.wait_send())
    for d in range(4):
        over_a(d).wait_send()
    for j in range(8):
        over_b(j).wait_send()
    for j in range(1, 16):
        back[j].wait_send()
    swap_hid.wait_send()
    for swap in swaps:
        swap.wait_send()
    for store in stores:
        store.wait()


def on_pair(grad_out, expert_ids, router_weights, saved_hidden, down_weight):
    tokens, features = grad_out.shape
    _, _, experts, capacity, hidden_units = saved_hidden.shape
    half = hidden_units // 2
    slots = experts * capacity
    bf16, f32 = jnp.bfloat16, jnp.float32
    dma = pltpu.SemaphoreType.DMA
    vmem = pl.BlockSpec(memory_space=pltpu.VMEM)
    hbm = pl.BlockSpec(memory_space=pl.ANY)
    grad_hidden, grad_weight, grad_router = pl.pallas_call(
        fused_kernel,
        out_shape=(
            jax.ShapeDtypeStruct((experts, capacity, hidden_units), bf16),
            jax.ShapeDtypeStruct((half, features), bf16),
            jax.ShapeDtypeStruct(expert_ids.shape[::-1], f32),
        ),
        in_specs=[vmem, vmem, hbm, hbm, hbm],
        out_specs=(hbm, hbm, vmem),
        scratch_shapes=[
            pltpu.VMEM((experts * tokens, features + META), bf16),
            pltpu.VMEM((experts, capacity, hidden_units), bf16),
            pltpu.VMEM((hidden_units, features), bf16),
            pltpu.VMEM((slots // 2, features), bf16),
            pltpu.VMEM((2 * slots, features), bf16),
            pltpu.VMEM((2, half, slots // 2), bf16),
            pltpu.VMEM((2, half, slots // 2), bf16),
            pltpu.VMEM((2, half, slots // 2), bf16),
            pltpu.VMEM((half, features), f32),
            pltpu.VMEM((experts, capacity, hidden_units), bf16),
            pltpu.VMEM((half, features), bf16),
            pltpu.VMEM((experts, 8, 128), f32),
            pltpu.VMEM((experts, 8, 128), f32),
            dma,
            dma((16,)),
            dma,
            dma((16,)),
            dma((features // TILE,)),
            dma((16,)),
            dma((16,)),
            dma((5,)),
            dma,
            dma,
            dma((2,)),
            dma((2,)),
            dma((16,)),
            dma((16,)),
        ],
        compiler_params=pltpu.CompilerParams(
            collective_id=0, has_side_effects=True, vmem_limit_bytes=58 * 1024 * 1024
        ),
        cost_estimate=pl.CostEstimate(
            flops=4 * slots * hidden_units * features,
            bytes_accessed=10_000_000,
            transcendentals=0,
        ),
    )(expert_ids.T, router_weights.T, grad_out, saved_hidden[0, 0], down_weight[0])
    return grad_hidden[None, None], grad_weight[None], grad_router.T


def solution(mesh):
    fused = mesh.shape["expert"] == 16 and mesh.shape["dp"] == 2
    placed = (
        P(("expert", "dp"), None),
        P(("expert", "dp"), None),
        P(("expert", "dp"), None),
        P("dp", "expert", None, None, None),
        P("expert", None, None),
    )
    return jax.shard_map(
        on_pair if fused else on_device,
        mesh=mesh,
        in_specs=placed,
        out_specs=(
            P("dp", "expert", None, None, None),
            P("expert", "dp", None),
            P(("expert", "dp"), None),
        ),
        check_vma=False,
    )
```

```python
import jax
import jax.numpy as jnp
from jax import lax
from jax.experimental import pallas as pl
from jax.experimental.pallas import tpu as pltpu
from jax.sharding import PartitionSpec as P


def on_device(grad_out, expert_ids, router_weights, saved_hidden, down_weight):
    experts = lax.axis_size("expert")
    groups = lax.axis_size("dp")
    token_count = grad_out.shape[0]
    top_count = expert_ids.shape[1]
    capacity = saved_hidden.shape[3]
    features = grad_out.shape[1]
    hidden_units = saved_hidden.shape[4]
    flat_ids = expert_ids.reshape(-1)
    onehot = (flat_ids[:, None] == jnp.arange(experts, dtype=jnp.int32)[None, :]).astype(jnp.int32)
    slot_rank = jnp.sum((jnp.cumsum(onehot, axis=0) - onehot) * onehot, axis=1)
    slot_index = flat_ids * capacity + slot_rank
    token_rows = jnp.repeat(grad_out, top_count, axis=0)
    outgoing = (
        jnp.zeros((experts * capacity, features), jnp.bfloat16).at[slot_index].set(token_rows)
    )
    outgoing = outgoing.reshape(experts, capacity, features)
    scales_out = (
        jnp.zeros((experts * capacity,), jnp.bfloat16)
        .at[slot_index]
        .set(router_weights.reshape(-1))
    )
    scales_out = scales_out.reshape(experts, capacity)
    arrived, arrived_scales = (
        lax.all_to_all(outgoing, "expert", split_axis=0, concat_axis=0, tiled=True),
        lax.all_to_all(scales_out, "expert", split_axis=0, concat_axis=0, tiled=True),
    )
    slot_rows = arrived.reshape(experts * capacity, features)
    row_scale = arrived_scales.reshape(-1).astype(jnp.float32)
    hidden_rows = saved_hidden.reshape(experts * capacity, hidden_units)
    weight = down_weight[0]
    projected = lax.dot_general(
        slot_rows, weight, (((1,), (1,)), ((), ())), preferred_element_type=jnp.float32
    )
    grad_hidden = (row_scale[:, None] * projected).astype(jnp.bfloat16)
    grad_hidden = grad_hidden.reshape(1, 1, experts, capacity, hidden_units)
    prob_grad = jnp.sum(hidden_rows.astype(jnp.float32) * projected, axis=1).reshape(
        experts, capacity
    )
    returned = lax.all_to_all(prob_grad, "expert", split_axis=0, concat_axis=0, tiled=True)
    grad_router = returned.reshape(-1)[slot_index].reshape(token_count, top_count)
    scaled = (row_scale[:, None] * slot_rows.astype(jnp.float32)).astype(jnp.bfloat16)
    own_rows = hidden_units // groups
    weight_term = lax.dot_general(
        hidden_rows, scaled, (((0,), (0,)), ((), ())), preferred_element_type=jnp.float32
    )
    weight_term = weight_term.astype(jnp.bfloat16).astype(jnp.float32)
    summed = lax.psum_scatter(
        weight_term.astype(jnp.bfloat16), "dp", scatter_dimension=0, tiled=True
    )
    grad_weight = summed.reshape(1, own_rows, features)
    return (grad_hidden, grad_weight, grad_router)


MESH = pl.DeviceIdType.MESH
META = 128
TILE = 256


def inverse(j):
    return (j // 4) * 4 + (4 - j % 4) % 4


def fused_kernel(
    ids_ref, rw_ref, go_hbm, hid_hbm, w_hbm,
    gh, gw, gr_ref,
    tok, hid, wv, x, sc, hid_own, hid_sib, hid_out, acc, msg, ret,
    go_sem, hid_sem, w_sem,
    tok_send, tok_recv, z_send, hid_send, hid_recv, sc_send, sc_recv, ret_send, ret_recv,
):
    f32, bf16 = jnp.float32, jnp.bfloat16
    tokens, features = go_hbm.shape
    capacity, hidden_units = hid.shape[1], hid.shape[2]
    half = hidden_units // 2
    slots = 8 * capacity
    rows = 8 * tokens
    me = lax.axis_index("expert")
    g = lax.axis_index("dp")
    stride_a, stride_b = 1 + g, 2 - g
    step_a = stride_a * (1 - 2 * ((me // stride_a) % 2))
    step_b = stride_b * (1 - 2 * ((me // stride_b) % 2))
    base = (me, me + step_a, me + step_b, me + step_a + step_b)
    source = [lax.rem(base[j // 4] + 16 - 4 * (j % 4), 16) for j in range(16)]
    next_a, next_b = base[1], base[2]

    barrier = pltpu.get_barrier_semaphore()
    for j in range(1, 16):
        pl.semaphore_signal(barrier, inc=1, device_id=(source[j], g), device_id_type=MESH)
    pl.semaphore_signal(barrier, inc=1, device_id=(me, 1 - g), device_id_type=MESH)

    load_go = pltpu.make_async_copy(go_hbm, tok.at[pl.ds(0, tokens), pl.ds(0, features)], go_sem)
    load_go.start()
    load_hid = []
    for j in range(16):
        load_hid.append(pltpu.make_async_copy(hid_hbm.at[source[j]], hid.at[j], hid_sem.at[j]))
        load_hid[j].start()
    load_w = pltpu.make_async_copy(w_hbm, wv, w_sem)
    load_w.start()

    ids = ids_ref[...]
    rw = rw_ref[...].astype(f32)
    place = lax.broadcasted_iota(jnp.int32, (META, tokens), 0)
    expert = place % 16
    weight = jnp.zeros((META, tokens), f32)
    routed = jnp.zeros((META, tokens), f32)
    for k in range(ids.shape[0]):
        hit = ids[k : k + 1, :] == expert
        weight += jnp.where(hit, rw[k : k + 1, :], 0.0)
        routed += jnp.where(hit, 1.0, 0.0)
    one = lax.broadcasted_iota(jnp.int32, (tokens, tokens), 0)
    two = lax.broadcasted_iota(jnp.int32, (tokens, tokens), 1)
    rank = jnp.dot(
        routed.astype(bf16), jnp.where(one < two, 1.0, 0.0).astype(bf16), preferred_element_type=f32
    )
    rank = jnp.where(routed > 0.0, rank + 1.0, 0.0)
    meta = jnp.where(place < 16, weight, jnp.where(place < 32, rank, 0.0))
    meta = lax.dot_general(
        jnp.where(one == two, 1.0, 0.0).astype(bf16),
        meta.astype(bf16),
        (((1,), (1,)), ((), ())),
        preferred_element_type=f32,
    )
    tok[pl.ds(0, tokens), pl.ds(features, META)] = meta.astype(bf16)
    msg[...] = jnp.zeros_like(msg)
    load_go.wait()
    pl.semaphore_wait(barrier, 16)

    part_rows = tokens // 2

    def block(src, dst, device, send, p):
        return pltpu.make_async_remote_copy(
            src_ref=tok.at[pl.ds(pl.multiple_of(src * tokens + p * part_rows, part_rows), part_rows)],
            dst_ref=tok.at[pl.ds(pl.multiple_of(dst * tokens + p * part_rows, part_rows), part_rows)],
            send_sem=send.at[p],
            recv_sem=tok_recv.at[dst, p],
            device_id=(device, g),
            device_id_type=MESH,
        )

    def over_a(d, p):
        return block(d, 4 + d, next_a, tok_send.at[4 + d], p)

    def over_b(j, p):
        return block(j, 8 + j, next_b, tok_send.at[8 + j], p)

    z = me // 4
    first, last = 1 - (z + 3) // 4, z // 3
    order = (1 + 2 * first, 3 - first - last, 2 + last - first)

    def along_z(act, p):
        @pl.when(z < 3)
        def _():
            act(block(0, 1, me + 4, z_send.at[0], p))

        @pl.when(z > 0)
        def _():
            act(block(0, 3, me - 4, z_send.at[4], p))

    def pass_on(d, act, p):
        @pl.when(jnp.logical_and(d <= z, z < 3))
        def _():
            act(block(d, d + 1, me + 4, z_send.at[d], p))

        @pl.when(jnp.logical_and(d > z, z > 0))
        def _():
            act(block(d, d - 1, me - 4, z_send.at[d], p))

    for p in range(2):
        along_z(lambda copy: copy.start(), p)
        over_a(0, p).start()
        over_b(0, p).start()

    for j in range(16):
        load_hid[j].wait()

    def turn(i, carry):
        at = pl.multiple_of(i * 128, 128)
        mine = pl.multiple_of(g * half + i * 128, 128)
        other = pl.multiple_of((1 - g) * half + i * 128, 128)
        for part in range(2):
            for col, ref in ((other, hid_out), (mine, hid_own)):
                piece = hid[pl.ds(8 * part, 8), :, pl.ds(col, 128)].astype(f32).reshape(slots, 128)
                ref[part, pl.ds(at, 128), :] = piece.T.astype(bf16)
        return carry

    lax.fori_loop(0, half // 128, turn, 0)
    swap_hid = pltpu.make_async_remote_copy(
        src_ref=hid_out,
        dst_ref=hid_sib,
        send_sem=hid_send,
        recv_sem=hid_recv,
        device_id=(me, 1 - g),
        device_id_type=MESH,
    )
    swap_hid.start()

    before = 0
    for d in order:
        for p in range(2):
            block(0, d, next_a, tok_send.at[0], p).wait_recv()
            pass_on(d, lambda copy: copy.start(), p)
            over_a(d, p).start()
            over_b(d, p).start()
            over_a(before, p).wait_recv()
            over_b(4 + before, p).start()
        before = d
    for p in range(2):
        over_a(before, p).wait_recv()
        over_b(4 + before, p).start()
    load_w.wait()

    back = [None] * 16
    swaps = []

    def work(part):
        at = part * rows
        lanes = lax.broadcasted_iota(jnp.int32, (rows, META), 1)
        held = tok[pl.ds(at, rows), pl.ds(features, META)].astype(f32)
        rank1 = jnp.sum(jnp.where(lanes == me + 16, held, 0.0), axis=1, keepdims=True)
        row = lax.broadcasted_iota(jnp.int32, (rows, 1), 0)
        first = ((row // tokens) * capacity).astype(f32)
        target = jnp.where(rank1 > 0.0, first + rank1 - 1.0, -1.0)
        eye = lax.broadcasted_iota(jnp.int32, (rows, rows), 0) == lax.broadcasted_iota(
            jnp.int32, (rows, rows), 1
        )
        target = jnp.sum(jnp.where(eye, target, 0.0), axis=0, keepdims=True)
        slot = lax.broadcasted_iota(jnp.int32, (slots, rows), 0).astype(f32)
        chosen = slot == target
        pick = jnp.where(chosen, 1.0, 0.0).astype(bf16)
        slot_meta = jnp.dot(
            pick, tok[pl.ds(at, rows), pl.ds(features, META)], preferred_element_type=f32
        )
        lanes = lax.broadcasted_iota(jnp.int32, (slots, META), 1)
        scale = jnp.sum(jnp.where(lanes == me, slot_meta, 0.0), axis=1, keepdims=True)
        for i in range(features // TILE):
            cols = pl.ds(i * TILE, TILE)
            moved = jnp.dot(pick, tok[pl.ds(at, rows), cols], preferred_element_type=f32)
            x[:, cols] = moved.astype(bf16)
            sc[pl.ds(part * slots, slots), cols] = (scale * moved).astype(bf16)
        swap = pltpu.make_async_remote_copy(
            src_ref=sc.at[pl.ds(part * slots, slots)],
            dst_ref=sc.at[pl.ds((2 + part) * slots, slots)],
            send_sem=sc_send.at[part],
            recv_sem=sc_recv.at[part],
            device_id=(me, 1 - g),
            device_id_type=MESH,
        )
        swap.start()
        swaps.append(swap)
        prob = jnp.zeros((slots, 1), f32)
        for i in range(hidden_units // TILE):
            cols = pl.ds(i * TILE, TILE)
            projected = lax.dot_general(
                x[...], wv[cols, :], (((1,), (1,)), ((), ())), preferred_element_type=f32
            )
            saved = hid[pl.ds(8 * part, 8), :, cols].astype(f32).reshape(slots, TILE)
            prob += jnp.sum(saved * projected, axis=1, keepdims=True)
            rows_out = (scale * projected).reshape(8, capacity, TILE).astype(bf16)
            for k in range(8):
                gh[source[8 * part + k], :, cols] = rows_out[k]
        by_token = jnp.sum(jnp.where(chosen, prob, 0.0), axis=0, keepdims=True)
        for i in range(8):
            j = 8 * part + i
            mine = by_token[:, tokens * i : tokens * (i + 1)]
            if j == 0:
                ret[0, 0:1, 0:tokens] = mine
            else:
                msg[j, 0:1, 0:tokens] = mine
        for i in range(8):
            j = 8 * part + i
            if j > 0:
                back[j] = pltpu.make_async_remote_copy(
                    src_ref=msg.at[j],
                    dst_ref=ret.at[inverse(j)],
                    send_sem=ret_send.at[j],
                    recv_sem=ret_recv.at[inverse(j)],
                    device_id=(source[j], g),
                    device_id_type=MESH,
                )
                back[j].start()

    def weight_part(part, cols):
        return jnp.dot(
            hid_own[part], sc[pl.ds(part * slots, slots), cols], preferred_element_type=f32
        ) + jnp.dot(
            hid_sib[part], sc[pl.ds((2 + part) * slots, slots), cols], preferred_element_type=f32
        )

    work(0)
    swap_hid.wait_recv()
    swaps[0].wait_recv()
    for i in range(features // TILE):
        cols = pl.ds(i * TILE, TILE)
        acc[:, cols] = weight_part(0, cols)
    for j in range(8):
        for p in range(2):
            over_b(j, p).wait_recv()
    work(1)
    swaps[1].wait_recv()
    for i in range(features // TILE):
        cols = pl.ds(i * TILE, TILE)
        gw[:, cols] = (acc[:, cols] + weight_part(1, cols)).astype(bf16)

    total = jnp.zeros(ids.shape, f32)
    for j in range(16):
        if j > 0:
            back[inverse(j)].wait_recv()
        total += jnp.where(ids == source[j], ret[j, 0:1, 0:tokens], 0.0)
    gr_ref[...] = total

    for p in range(2):
        along_z(lambda copy: copy.wait_send(), p)
        for d in order:
            pass_on(d, lambda copy: copy.wait_send(), p)
        for d in range(4):
            over_a(d, p).wait_send()
        for j in range(8):
            over_b(j, p).wait_send()
    for j in range(1, 16):
        back[j].wait_send()
    swap_hid.wait_send()
    for swap in swaps:
        swap.wait_send()


def on_pair(grad_out, expert_ids, router_weights, saved_hidden, down_weight):
    tokens, features = grad_out.shape
    _, _, experts, capacity, hidden_units = saved_hidden.shape
    half = hidden_units // 2
    slots = experts * capacity
    bf16, f32 = jnp.bfloat16, jnp.float32
    dma = pltpu.SemaphoreType.DMA
    vmem = pl.BlockSpec(memory_space=pltpu.VMEM)
    hbm = pl.BlockSpec(memory_space=pl.ANY)
    grad_hidden, grad_weight, grad_router = pl.pallas_call(
        fused_kernel,
        out_shape=(
            jax.ShapeDtypeStruct((experts, capacity, hidden_units), bf16),
            jax.ShapeDtypeStruct((half, features), bf16),
            jax.ShapeDtypeStruct(expert_ids.shape[::-1], f32),
        ),
        in_specs=[vmem, vmem] + [pl.BlockSpec(memory_space=pltpu.HBM)] * 3,
        out_specs=(vmem, vmem, vmem),
        scratch_shapes=[
            pltpu.VMEM((experts * tokens, features + META), bf16),
            pltpu.VMEM((experts, capacity, hidden_units), bf16),
            pltpu.VMEM((hidden_units, features), bf16),
            pltpu.VMEM((slots // 2, features), bf16),
            pltpu.VMEM((2 * slots, features), bf16),
            pltpu.VMEM((2, half, slots // 2), bf16),
            pltpu.VMEM((2, half, slots // 2), bf16),
            pltpu.VMEM((2, half, slots // 2), bf16),
            pltpu.VMEM((half, features), f32),
            pltpu.VMEM((experts, 8, 128), f32),
            pltpu.VMEM((experts, 8, 128), f32),
            dma,
            dma((16,)),
            dma,
            dma((16, 2)),
            dma((16, 2)),
            dma((5, 2)),
            dma,
            dma,
            dma((2,)),
            dma((2,)),
            dma((16,)),
            dma((16,)),
        ],
        compiler_params=pltpu.CompilerParams(
            collective_id=0, has_side_effects=True, vmem_limit_bytes=48 * 1024 * 1024
        ),
        cost_estimate=pl.CostEstimate(
            flops=4 * slots * hidden_units * features,
            bytes_accessed=10_000_000,
            transcendentals=0,
        ),
    )(expert_ids.T, router_weights.T, grad_out, saved_hidden[0, 0], down_weight[0])
    return grad_hidden[None, None], grad_weight[None], grad_router.T


def solution(mesh):
    fused = mesh.shape["expert"] == 16 and mesh.shape["dp"] == 2
    placed = (
        P(("expert", "dp"), None),
        P(("expert", "dp"), None),
        P(("expert", "dp"), None),
        P("dp", "expert", None, None, None),
        P("expert", None, None),
    )
    return jax.shard_map(
        on_pair if fused else on_device,
        mesh=mesh,
        in_specs=placed,
        out_specs=(
            P("dp", "expert", None, None, None),
            P("expert", "dp", None),
            P(("expert", "dp"), None),
        ),
        check_vma=False,
    )
```
